32 devices in a mesh: packs: 2 (over x), rows: 16 (over z, y, core).
Axes of the slice: x: 2, y: 2, z: 4, core: 2. Of those that a mesh axis runs over, the one named last changes fastest.
Arguments:
- start_slab: bfloat16 [131072, 256], P(('packs', 'rows')), parts along dimension 0, may hold values from -6 to 6
- blocks: bfloat16 [1024, 8, 128, 128], P(('packs', 'rows')), parts along dimension 0
- couple: int32 [1024, 8], P(('packs', 'rows')), parts along dimension 0, may hold values from 0 to 47, as said below
- counts: int32 [1024], P(('packs', 'rows')), parts along dimension 0, may hold values from 1 to 8, as said below
- send_blocks: int32 [32, 2, 8], P(('packs', 'rows')), parts along dimension 0, may hold values from 0 to 31, as said below
- center: float32 [3], replicated, may hold values from 1.5 to 3
- halfwidth: float32 [3], replicated, may hold values from 1.5 to 3
Outputs:
- basis: float32 [131072, 256], P(('packs', 'rows')), parts along dimension 0
- projected: float32 [512, 256], P('packs'), parts along dimension 0
The draws below stay inside these ranges and needn't reach their ends.
There are 2 independent parts, one for each index of `packs`. The reference program is written for one: setup_inputs(seed, part) draws one part's arguments, and reference() takes and returns one part's arrays. A program takes and returns all parts, laid end to end along the dimension named above; an argument that names none is the same for every part. Nothing has to cross between parts.
Inputs may be any that keep to these rules, and one draw needn't show every extreme that they name: couple[r, 0] is r's own local block row r mod 32; other entries are any slot. `counts`: each block row has the diagonal slot live; every device has a block row with all 8 slots live. `send_blocks`: distinct local block rows in each list.
All inputs are finite; a program needn't handle non-finite values.
Results may differ from the reference program's by a relative error of at most 0.00095.
The reference program's roundings to bfloat16 on the way count: a program that leaves them out, or rounds other values in their place, can miss the bound.
Values may be sent and summed in bfloat16 or wider, within the bound.
A program may use at most 128 MiB of HBM per device.

```python
import jax
import jax.numpy as jnp
from jax import lax

BLK = 128
SUB = 256
NB = 8
STEPS = 3
RB_DEV = 32
SMAX = 8
EXT = 48
ROW_BLOCKS = 512
TOTAL_ROWS = 65536
N_ROWS = 16


def draw_blocks(key, part):
    key = jax.random.fold_in(key, 11)
    noise_key, diag_key = jax.random.split(key)
    shape = (ROW_BLOCKS, NB, BLK, BLK)
    noise = jax.random.normal(noise_key, shape, jnp.float32)
    diag = jnp.exp(jax.random.uniform(diag_key, (ROW_BLOCKS, BLK), jnp.float32, 0.4, 1.4))
    noise = noise / jnp.sqrt(jnp.float32(BLK * NB))
    identity = (jnp.arange(BLK)[:, None] == jnp.arange(BLK)[None, :]).astype(jnp.float32)
    first_slot = (jnp.arange(NB) == 0).astype(jnp.float32)
    values = noise + first_slot[None, :, None, None] * identity[None, None] * diag[:, None, :, None]
    return values.astype(jnp.bfloat16)


def draw_couple(key, part):
    key = jax.random.fold_in(key, 12)
    others = jax.random.randint(key, (ROW_BLOCKS, NB - 1), 0, EXT, dtype=jnp.int32)
    others = others.at[0::RB_DEV, 0].set(EXT - 1)
    own = (jnp.arange(ROW_BLOCKS, dtype=jnp.int32) % RB_DEV)[:, None]
    return jnp.concatenate([own, others], axis=1).astype(jnp.int32)


def draw_counts(key, part):
    key = jax.random.fold_in(key, 13)
    values = jax.random.randint(key, (ROW_BLOCKS,), 1, NB + 1, dtype=jnp.int32)
    values = values.at[0::RB_DEV].set(NB)
    values = values.at[1::RB_DEV].set(1)
    return values


def draw_send_blocks(key, part):
    key = jax.random.fold_in(key, 14)
    devices = ROW_BLOCKS // RB_DEV
    scores = jax.random.randint(key, (devices, 2, RB_DEV), 0, 2 ** 20, dtype=jnp.int32)
    scores = scores * RB_DEV + jnp.arange(RB_DEV, dtype=jnp.int32)[None, None, :]
    order = jnp.argsort(scores, axis=-1)
    return order[:, :, :SMAX].astype(jnp.int32)


def levels(key, dims, pieces, smallest, top_value):
    def one(dim, parts):
        heights = jax.random.uniform(jax.random.fold_in(jax.random.fold_in(key, 6), dim), (parts,), jnp.float32, smallest / len(pieces), top_value / len(pieces))
        return jnp.repeat(jnp.exp(heights), dims[dim] // parts).reshape((-1,) + (1,) * (len(dims) - dim - 1))

    gain = one(*pieces[0])
    for cut in pieces[1:]:
        gain = gain * one(*cut)
    return gain


def gaussian(own_key, dims, scale, limit, cuts=(), held_as=jnp.bfloat16):
    entries = jax.random.normal(own_key, dims, jnp.float32) * scale
    if len(cuts) > 0:
        entries = levels(own_key, dims, cuts, -0.22, 0.18) * entries
    return jnp.clip(entries, min=-limit, max=limit).astype(held_as)


def setup_inputs(seed: int = 0, part: int = 0) -> dict:
    arg_keys = jax.random.split(jax.random.key(seed), 8)
    own_keys = jax.random.split(jax.random.fold_in(arg_keys[7], part), 8)
    return {
        "start_slab": gaussian(own_keys[0], (TOTAL_ROWS, SUB), 1.0, 6.0, ((0, 16),)),
        "blocks": draw_blocks(jax.random.fold_in(jax.random.fold_in(arg_keys[7], part), 71), part),
        "couple": draw_couple(jax.random.fold_in(jax.random.fold_in(arg_keys[7], part), 71), part),
        "counts": draw_counts(jax.random.fold_in(jax.random.fold_in(arg_keys[7], part), 71), part),
        "send_blocks": draw_send_blocks(jax.random.fold_in(jax.random.fold_in(arg_keys[7], part), 71), part),
        "center": jnp.clip(jax.random.uniform(arg_keys[5], (STEPS,), jnp.float32, 1.5, 3.0), 1.5, 3.0),
        "halfwidth": jnp.clip(jax.random.uniform(arg_keys[6], (STEPS,), jnp.float32, 1.5, 3.0), 1.5, 3.0),
    }


def slot_table(send_blocks):
    device_ids = jnp.arange(N_ROWS, dtype=jnp.int32)
    own_index = device_ids[:, None] * RB_DEV + jnp.arange(RB_DEV, dtype=jnp.int32)[None, :]
    below_lists = send_blocks[jnp.clip(device_ids - 1, 0, N_ROWS - 1), 1]
    above_lists = send_blocks[jnp.clip(device_ids + 1, 0, N_ROWS - 1), 0]
    below_index = jnp.where(device_ids[:, None] > 0, (device_ids[:, None] - 1) * RB_DEV + below_lists, ROW_BLOCKS)
    above_index = jnp.where(device_ids[:, None] < N_ROWS - 1, (device_ids[:, None] + 1) * RB_DEV + above_lists, ROW_BLOCKS)
    return jnp.concatenate([own_index, below_index, above_index], axis=1).astype(jnp.int32)

def conduct(slab_blocks, blocks, couple, counts, global_slots):
    padded = jnp.concatenate([slab_blocks, jnp.zeros((1, BLK, SUB), jnp.bfloat16)], axis=0)
    active = (jnp.arange(NB, dtype=jnp.int32)[None, :] < counts[:, None]).astype(jnp.bfloat16)

    def per_device(device):
        start_row = (device * RB_DEV).astype(jnp.int32)
        couple_here = lax.dynamic_slice_in_dim(couple, start_row, RB_DEV, 0)
        block_here = lax.dynamic_slice_in_dim(blocks, start_row, RB_DEV, 0)
        active_here = lax.dynamic_slice_in_dim(active, start_row, RB_DEV, 0)
        slots_here = global_slots[device]
        gathered = padded[slots_here[couple_here]]
        masked = block_here * active_here[:, :, None, None]
        return jnp.einsum('rkij,rkjc->ric', masked.astype(jnp.float32), gathered.astype(jnp.float32))
    result = lax.map(per_device, jnp.arange(N_ROWS, dtype=jnp.int32))
    return result.reshape(ROW_BLOCKS, BLK, SUB)

def reference(start_slab, blocks, couple, counts, send_blocks, center, halfwidth):
    global_slots = slot_table(send_blocks)
    current = start_slab.reshape(ROW_BLOCKS, BLK, SUB)
    for filter_step in range(STEPS):
        product = conduct(current, blocks, couple, counts, global_slots)
        current = ((product - center[filter_step] * current.astype(jnp.float32)) / halfwidth[filter_step]).astype(jnp.bfloat16)
    image = conduct(current, blocks, couple, counts, global_slots).astype(jnp.bfloat16)
    flat = current.reshape(TOTAL_ROWS, SUB)
    image_flat = image.reshape(TOTAL_ROWS, SUB)
    gram = jnp.dot(flat.T.astype(jnp.float32), flat.astype(jnp.float32), preferred_element_type=jnp.float32) / TOTAL_ROWS
    moment = jnp.dot(flat.T.astype(jnp.float32), image_flat.astype(jnp.float32), preferred_element_type=jnp.float32) / TOTAL_ROWS
    factor = jnp.linalg.cholesky(gram)
    basis = lax.linalg.triangular_solve(factor, flat.astype(jnp.float32), left_side=False, lower=True, transpose_a=True)
    left_solved = lax.linalg.triangular_solve(factor, moment, left_side=True, lower=True)
    projected = lax.linalg.triangular_solve(factor, left_solved, left_side=False, lower=True, transpose_a=True)
    return (basis, projected)
```

```python
import functools

import jax
import jax.numpy as jnp
from jax import lax
from jax.experimental import pallas as pl
from jax.experimental.pallas import tpu as pltpu
from jax.sharding import PartitionSpec as P

STEPS = 3
PANEL = 16
CHUNK = 512
F32 = jnp.float32
BF16 = jnp.bfloat16
HIGHEST = lax.Precision.HIGHEST


def filter_kernel(
    devices,
    total_rows,
    couple_ref,
    counts_ref,
    send_ref,
    center_ref,
    inverse_ref,
    start_ref,
    blocks_hbm,
    slab_out,
    sums_out,
    blocks_ref,
    own_a,
    own_b,
    ext_a,
    ext_b,
    up_a,
    up_b,
    down_a,
    down_b,
    slab_t,
    sums,
    arrived,
    total,
    load_sem,
    send_sem,
    recv_sem,
    sum_send_sem,
    sum_recv_sem,
):
    rows = blocks_ref.shape[0]
    slots = blocks_ref.shape[1]
    size = blocks_ref.shape[2]
    columns = slab_t.shape[0]
    lists = send_ref.shape[1]
    me = lax.axis_index("rows")
    levels = devices.bit_length() - 1

    def partner(level):
        distance = 1 << level
        bit = (me // distance) % 2
        return me + distance * (1 - 2 * bit), bit

    load = pltpu.make_async_copy(blocks_hbm, blocks_ref, load_sem)
    load.start()

    barrier = pltpu.get_barrier_semaphore()

    @pl.when(me > 0)
    def _():
        pl.semaphore_signal(barrier, inc=1, device_id={"rows": me - 1}, device_id_type=pl.DeviceIdType.MESH)

    @pl.when(me < devices - 1)
    def _():
        pl.semaphore_signal(barrier, inc=1, device_id={"rows": me + 1}, device_id_type=pl.DeviceIdType.MESH)

    for level in range(levels):
        pl.semaphore_signal(barrier, inc=1, device_id={"rows": partner(level)[0]}, device_id_type=pl.DeviceIdType.MESH)

    for ext in (ext_a, ext_b):
        @pl.when(me == 0)
        def _():
            ext[rows : rows + lists] = jnp.zeros((lists, size, columns), BF16)

        @pl.when(me == devices - 1)
        def _():
            ext[rows + lists : rows + 2 * lists] = jnp.zeros((lists, size, columns), BF16)

    @pl.loop(0, rows)
    def _(r):
        ext_a[r] = start_ref[r]

    ends = (me == 0).astype(jnp.int32) + (me == devices - 1).astype(jnp.int32)
    pl.semaphore_wait(barrier, levels + 2 - ends)

    def exchange(step):
        own = start_ref if step == 0 else (own_a, own_b)[step % 2]
        ext = (ext_a, ext_b)[step % 2]
        up = (up_a, up_b)[step % 2]
        down = (down_a, down_b)[step % 2]
        to_up = pltpu.make_async_remote_copy(
            src_ref=up,
            dst_ref=ext.at[pl.ds(rows, lists)],
            send_sem=send_sem.at[step, 0],
            recv_sem=recv_sem.at[step, 0],
            device_id={"rows": me + 1},
            device_id_type=pl.DeviceIdType.MESH,
        )
        to_down = pltpu.make_async_remote_copy(
            src_ref=down,
            dst_ref=ext.at[pl.ds(rows + lists, lists)],
            send_sem=send_sem.at[step, 1],
            recv_sem=recv_sem.at[step, 1],
            device_id={"rows": me - 1},
            device_id_type=pl.DeviceIdType.MESH,
        )

        def start():
            @pl.when(me < devices - 1)
            def _():
                for j in range(lists):
                    up[j] = own[send_ref[1, j]]
                to_up.start()

            @pl.when(me > 0)
            def _():
                for j in range(lists):
                    down[j] = own[send_ref[0, j]]
                to_down.start()

        def finish():
            @pl.when(me < devices - 1)
            def _():
                to_up.wait_send()
                to_down.wait_recv()

            @pl.when(me > 0)
            def _():
                to_down.wait_send()
                to_up.wait_recv()

        return start, finish

    def conduct(ext, r):
        live = counts_ref[r]
        left, right = [], []
        for k in range(slots):
            block = blocks_ref[r, k]
            left.append(jnp.where(k < live, block, jnp.zeros_like(block)))
            right.append(ext[couple_ref[r, k]])
        return jnp.dot(
            jnp.concatenate(left, axis=1), jnp.concatenate(right, axis=0), preferred_element_type=F32
        )

    for step in range(STEPS + 1):
        start, finish = exchange(step)
        start()
        ext = (ext_a, ext_b)[step % 2]
        own = start_ref if step == 0 else (own_a, own_b)[step % 2]
        if step == 0:
            load.wait()
        if step == STEPS:
            sums[...] = jnp.zeros_like(sums)
            per = CHUNK // size

            @pl.loop(0, rows // per)
            def _(c):
                part = own[pl.ds(c * per, per)].reshape(CHUNK, columns)
                part_t = part.T
                slab_t[:, pl.ds(pl.multiple_of(c * CHUNK, CHUNK), CHUNK)] = part_t
                sums[0:columns] += jnp.dot(part_t, part, preferred_element_type=F32)
                slab_out[pl.ds(c * per, per)] = own[pl.ds(c * per, per)]
        finish()
        if step < STEPS:
            own_next = (own_b, own_a)[step % 2]
            ext_next = (ext_b, ext_a)[step % 2]

            @pl.loop(0, rows)
            def _(r):
                product = conduct(ext, r)
                new = ((product - center_ref[step] * own[r].astype(F32)) * inverse_ref[step]).astype(BF16)
                own_next[r] = new
                ext_next[r] = new
        else:
            image = own_a if step % 2 else own_b

            @pl.loop(0, rows)
            def _(r):
                image[r] = conduct(ext, r).astype(BF16)

            @pl.loop(0, rows // per)
            def _(c):
                part = image[pl.ds(c * per, per)].reshape(CHUNK, columns)
                part_t = slab_t[:, pl.ds(pl.multiple_of(c * CHUNK, CHUNK), CHUNK)]
                sums[columns : 2 * columns] += jnp.dot(part_t, part, preferred_element_type=F32)

    offset = 0
    length = 2 * columns
    spans = []
    at = 0
    for level in range(levels):
        other, bit = partner(level)
        length //= 2
        keep = pl.multiple_of(offset + bit * length, length)
        give = pl.multiple_of(offset + (1 - bit) * length, length)
        copy = pltpu.make_async_remote_copy(
            src_ref=sums.at[pl.ds(give, length)],
            dst_ref=arrived.at[pl.ds(at, length)],
            send_sem=sum_send_sem.at[0, level],
            recv_sem=sum_recv_sem.at[0, level],
            device_id={"rows": other},
            device_id_type=pl.DeviceIdType.MESH,
        )
        copy.start()
        copy.wait()
        sums[pl.ds(keep, length)] += arrived[pl.ds(at, length)]
        spans.append((other, keep, length))
        offset = keep
        at += length
    total[pl.ds(offset, length)] = sums[pl.ds(offset, length)]
    for level in reversed(range(levels)):
        other, keep, length = spans[level]
        copy = pltpu.make_async_remote_copy(
            src_ref=total.at[pl.ds(keep, length)],
            dst_ref=total.at[pl.ds(keep, length)],
            send_sem=sum_send_sem.at[1, level],
            recv_sem=sum_recv_sem.at[1, level],
            device_id={"rows": other},
            device_id_type=pl.DeviceIdType.MESH,
        )
        copy.start()
        copy.wait()
    sums_out[...] = total[...] / total_rows


def invert_factor(work):
    order = work.shape[0]
    half = order // 2
    inside = lax.broadcasted_iota(jnp.int32, (PANEL, 1), 0)
    for p in range(order // PANEL):
        base, end = p * PANEL, (p + 1) * PANEL
        low = (base // half) * half
        top = low + half
        wide = work[base:end, low : order + top]
        column = [
            jnp.broadcast_to(work[base:end, base + k : base + k + 1], (PANEL, 128)) for k in range(PANEL)
        ]
        width = order + top - low
        inverse = []
        for j in range(PANEL):
            pivot = 1.0 / column[j][j : j + 1, :]
            inverse.append(pivot)
            if j < PANEL - 1:
                factor = jnp.where(inside > j, column[j] * pivot, 0.0)
                for k in range(j + 1, PANEL):
                    column[k] = column[k] - factor * column[k][j : j + 1, :]
                wide = wide - jnp.tile(factor, (1, width // 128)) * wide[j : j + 1, :]
        inverse = jnp.concatenate(inverse, axis=0)
        if end < order:
            first = (end // half) * half
            scaled = wide[:, first - low : order - low] * jnp.tile(inverse, (1, (order - first) // 128))
            ids = lax.broadcasted_iota(jnp.int32, scaled.shape, 1) + first
            scaled = jnp.where(ids >= end, scaled, 0.0)
            work[first:order, low : order + top] -= lax.dot_general(
                scaled, wide, (((0,), (0,)), ((), ())), precision=HIGHEST, preferred_element_type=F32
            )
        root = jnp.sqrt(inverse)
        work[base:end, order : order + top] = wide[:, order - low :] * jnp.tile(root, (1, top // 128))


def basis_kernel(slab_ref, sums_ref, basis_ref, projected_ref, work, high, low):
    order = slab_ref.shape[1]

    @pl.when(pl.program_id(0) == 0)
    def _():
        rows = lax.broadcasted_iota(jnp.int32, (order, order), 0)
        lanes = lax.broadcasted_iota(jnp.int32, (order, order), 1)
        work[:, 0:order] = sums_ref[0:order]
        work[:, order : 2 * order] = (rows == lanes).astype(F32)
        invert_factor(work)
        inverse = work[:, order : 2 * order]
        left = jnp.dot(inverse, sums_ref[order : 2 * order], precision=HIGHEST, preferred_element_type=F32)
        flipped = inverse.T
        projected_ref[...] = jnp.dot(left, flipped, precision=HIGHEST, preferred_element_type=F32)
        top = flipped.astype(BF16)
        high[...] = top
        low[...] = (flipped - top.astype(F32)).astype(BF16)

    slab = slab_ref[...]
    basis_ref[...] = jnp.dot(slab, high[...], preferred_element_type=F32) + jnp.dot(
        slab, low[...], preferred_element_type=F32
    )


def body(start_slab, blocks, couple, counts, send_blocks, center, halfwidth):
    rows, slots, size, _ = blocks.shape
    columns = start_slab.shape[1]
    local = start_slab.shape[0]
    lists = send_blocks.shape[2]
    devices = lax.axis_size("rows")
    total_rows = local * devices
    levels = devices.bit_length() - 1
    smem = pl.BlockSpec(memory_space=pltpu.SMEM)
    vmem = pl.BlockSpec(memory_space=pltpu.VMEM)
    own = pltpu.VMEM((rows, size, columns), BF16)
    ext = pltpu.VMEM((rows + 2 * lists, size, columns), BF16)
    listed = pltpu.VMEM((lists, size, columns), BF16)
    slab, sums = pl.pallas_call(
        functools.partial(filter_kernel, devices, float(total_rows)),
        out_shape=(
            jax.ShapeDtypeStruct((rows, size, columns), BF16),
            jax.ShapeDtypeStruct((2 * columns, columns), F32),
        ),
        in_specs=[smem] * 5 + [vmem, pl.BlockSpec(memory_space=pl.ANY)],
        out_specs=(vmem, vmem),
        scratch_shapes=[
            pltpu.VMEM(blocks.shape, BF16),
            own,
            own,
            ext,
            ext,
            listed,
            listed,
            listed,
            listed,
            pltpu.VMEM((columns, local), BF16),
            pltpu.VMEM((2 * columns, columns), F32),
            pltpu.VMEM((2 * columns, columns), F32),
            pltpu.VMEM((2 * columns, columns), F32),
            pltpu.SemaphoreType.DMA,
            pltpu.SemaphoreType.DMA((STEPS + 1, 2)),
            pltpu.SemaphoreType.DMA((STEPS + 1, 2)),
            pltpu.SemaphoreType.DMA((2, levels)),
            pltpu.SemaphoreType.DMA((2, levels)),
        ],
        compiler_params=pltpu.CompilerParams(
            collective_id=0, has_side_effects=True, vmem_limit_bytes=48 * 1024 * 1024
        ),
    )(
        couple,
        counts,
        send_blocks[0],
        center,
        1.0 / halfwidth,
        start_slab.reshape(rows, size, columns),
        blocks,
    )
    tile = 512
    return pl.pallas_call(
        basis_kernel,
        grid=(local // tile,),
        out_shape=(
            jax.ShapeDtypeStruct((local, columns), F32),
            jax.ShapeDtypeStruct((columns, columns), F32),
        ),
        in_specs=[
            pl.BlockSpec((tile, columns), lambda i: (i, 0)),
            pl.BlockSpec((2 * columns, columns), lambda i: (0, 0)),
        ],
        out_specs=(
            pl.BlockSpec((tile, columns), lambda i: (i, 0)),
            pl.BlockSpec((columns, columns), lambda i: (0, 0)),
        ),
        scratch_shapes=[
            pltpu.VMEM((columns, 2 * columns), F32),
            pltpu.VMEM((columns, columns), BF16),
            pltpu.VMEM((columns, columns), BF16),
        ],
        compiler_params=pltpu.CompilerParams(vmem_limit_bytes=32 * 1024 * 1024),
    )(slab.reshape(local, columns), sums)


def solution(mesh):
    return jax.shard_map(
        body,
        mesh=mesh,
        in_specs=(
            P(("packs", "rows"), None),
            P(("packs", "rows"), None, None, None),
            P(("packs", "rows"), None),
            P(("packs", "rows")),
            P(("packs", "rows"), None, None),
            P(),
            P(),
        ),
        out_specs=(P(("packs", "rows"), None), P("packs", None)),
        check_vma=False,
    )
```

```python
import functools

import jax
import jax.numpy as jnp
from jax import lax
from jax.experimental import pallas as pl
from jax.experimental.pallas import tpu as pltpu
from jax.sharding import PartitionSpec as P

STEPS = 3
PANEL = 16
CHUNK = 512
F32 = jnp.float32
BF16 = jnp.bfloat16
HIGHEST = lax.Precision.HIGHEST


def filter_kernel(
    devices,
    total_rows,
    table_hbm,
    scale_hbm,
    start_ref,
    blocks_hbm,
    slab_out,
    moment_out,
    inverse_out,
    high_out,
    low_out,
    blocks_ref,
    table,
    scale,
    work,
    own_a,
    own_b,
    ext_a,
    ext_b,
    up_a,
    up_b,
    down_a,
    down_b,
    slab_t,
    sums,
    arrived,
    total,
    load_sem,
    table_sem,
    send_sem,
    recv_sem,
    sum_send_sem,
    sum_recv_sem,
):
    rows = blocks_ref.shape[0]
    slots = blocks_ref.shape[1]
    size = blocks_ref.shape[2]
    columns = slab_t.shape[0]
    lists = (ext_a.shape[0] - rows) // 2
    counts_at = rows * slots
    send_at = counts_at + rows
    me = lax.axis_index("rows")
    levels = devices.bit_length() - 1

    def partner(level):
        distance = 1 << level
        bit = (me // distance) % 2
        return me + distance * (1 - 2 * bit), bit

    load = pltpu.make_async_copy(blocks_hbm, blocks_ref, load_sem)
    load.start()
    tables = (
        pltpu.make_async_copy(table_hbm, table, table_sem.at[0]),
        pltpu.make_async_copy(scale_hbm, scale, table_sem.at[1]),
    )
    for copy in tables:
        copy.start()

    barrier = pltpu.get_barrier_semaphore()

    @pl.when(me > 0)
    def _():
        pl.semaphore_signal(barrier, inc=1, device_id={"rows": me - 1}, device_id_type=pl.DeviceIdType.MESH)

    @pl.when(me < devices - 1)
    def _():
        pl.semaphore_signal(barrier, inc=1, device_id={"rows": me + 1}, device_id_type=pl.DeviceIdType.MESH)

    for level in range(levels):
        pl.semaphore_signal(barrier, inc=1, device_id={"rows": partner(level)[0]}, device_id_type=pl.DeviceIdType.MESH)

    for ext in (ext_a, ext_b):
        @pl.when(me == 0)
        def _():
            ext[rows : rows + lists] = jnp.zeros((lists, size, columns), BF16)

        @pl.when(me == devices - 1)
        def _():
            ext[rows + lists : rows + 2 * lists] = jnp.zeros((lists, size, columns), BF16)

    @pl.loop(0, rows)
    def _(r):
        ext_a[r] = start_ref[r]

    for copy in tables:
        copy.wait()
    ends = (me == 0).astype(jnp.int32) + (me == devices - 1).astype(jnp.int32)
    pl.semaphore_wait(barrier, levels + 2 - ends)

    def exchange(step):
        own = start_ref if step == 0 else (own_a, own_b)[step % 2]
        ext = (ext_a, ext_b)[step % 2]
        up = (up_a, up_b)[step % 2]
        down = (down_a, down_b)[step % 2]
        to_up = pltpu.make_async_remote_copy(
            src_ref=up,
            dst_ref=ext.at[pl.ds(rows, lists)],
            send_sem=send_sem.at[step, 0],
            recv_sem=recv_sem.at[step, 0],
            device_id={"rows": me + 1},
            device_id_type=pl.DeviceIdType.MESH,
        )
        to_down = pltpu.make_async_remote_copy(
            src_ref=down,
            dst_ref=ext.at[pl.ds(rows + lists, lists)],
            send_sem=send_sem.at[step, 1],
            recv_sem=recv_sem.at[step, 1],
            device_id={"rows": me - 1},
            device_id_type=pl.DeviceIdType.MESH,
        )

        def start():
            @pl.when(me < devices - 1)
            def _():
                for j in range(lists):
                    up[j] = own[table[send_at + lists + j]]
                to_up.start()

            @pl.when(me > 0)
            def _():
                for j in range(lists):
                    down[j] = own[table[send_at + j]]
                to_down.start()

        def finish():
            @pl.when(me < devices - 1)
            def _():
                to_up.wait_send()
                to_down.wait_recv()

            @pl.when(me > 0)
            def _():
                to_down.wait_send()
                to_up.wait_recv()

        return start, finish

    def conduct(ext, r):
        live = table[counts_at + r]
        left, right = [], []
        for k in range(slots):
            block = blocks_ref[r, k]
            left.append(jnp.where(k < live, block, jnp.zeros_like(block)))
            right.append(ext[table[r * slots + k]])
        return jnp.dot(
            jnp.concatenate(left, axis=1), jnp.concatenate(right, axis=0), preferred_element_type=F32
        )

    def reduction(which):
        phases = []
        offset = which * columns
        length = columns
        at = which * columns
        spans = []
        for level in range(levels):
            other, bit = partner(level)
            length //= 2
            keep = pl.multiple_of(offset + bit * length, length)
            give = pl.multiple_of(offset + (1 - bit) * length, length)
            copy = pltpu.make_async_remote_copy(
                src_ref=sums.at[pl.ds(give, length)],
                dst_ref=arrived.at[pl.ds(at, length)],
                send_sem=sum_send_sem.at[which, level],
                recv_sem=sum_recv_sem.at[which, level],
                device_id={"rows": other},
                device_id_type=pl.DeviceIdType.MESH,
            )

            def finish(copy=copy, keep=keep, at=at, length=length, last=level == levels - 1):
                copy.wait()
                here = pl.ds(keep, length)
                (total if last else sums)[here] = sums[here] + arrived[pl.ds(at, length)]

            phases.append((copy.start, finish))
            spans.append((other, keep, length))
            offset = keep
            at += length
        for level in reversed(range(levels)):
            other, keep, length = spans[level]
            copy = pltpu.make_async_remote_copy(
                src_ref=total.at[pl.ds(keep, length)],
                dst_ref=total.at[pl.ds(keep, length)],
                send_sem=sum_send_sem.at[which, levels + level],
                recv_sem=sum_recv_sem.at[which, levels + level],
                device_id={"rows": other},
                device_id_type=pl.DeviceIdType.MESH,
            )
            phases.append((copy.start, copy.wait))
        return phases

    for step in range(STEPS + 1):
        start, finish = exchange(step)
        start()
        ext = (ext_a, ext_b)[step % 2]
        own = start_ref if step == 0 else (own_a, own_b)[step % 2]
        if step == 0:
            load.wait()
        if step == STEPS:
            sums[...] = jnp.zeros_like(sums)
            per = CHUNK // size

            @pl.loop(0, rows // per)
            def _(c):
                part = own[pl.ds(c * per, per)].reshape(CHUNK, columns)
                part_t = part.T
                slab_t[:, pl.ds(pl.multiple_of(c * CHUNK, CHUNK), CHUNK)] = part_t
                sums[0:columns] += jnp.dot(part_t, part, preferred_element_type=F32)
                slab_out[pl.ds(c * per, per)] = own[pl.ds(c * per, per)]

            gram_phases = reduction(0)
            gram_phases[0][0]()
            gram_phases[0][1]()
            gram_phases[1][0]()
        finish()
        if step < STEPS:
            own_next = (own_b, own_a)[step % 2]
            ext_next = (ext_b, ext_a)[step % 2]

            @pl.loop(0, rows)
            def _(r):
                product = conduct(ext, r)
                new = ((product - scale[step] * own[r].astype(F32)) * scale[STEPS + step]).astype(BF16)
                own_next[r] = new
                ext_next[r] = new
        else:
            image = own_a if step % 2 else own_b

            groups = len(gram_phases) - 1
            for group in range(groups):
                @pl.loop(group * rows // groups, (group + 1) * rows // groups)
                def _(r):
                    image[r] = conduct(ext, r).astype(BF16)

                gram_phases[group + 1][1]()
                if group < groups - 1:
                    gram_phases[group + 2][0]()

            @pl.loop(0, rows // per)
            def _(c):
                part = image[pl.ds(c * per, per)].reshape(CHUNK, columns)
                part_t = slab_t[:, pl.ds(pl.multiple_of(c * CHUNK, CHUNK), CHUNK)]
                sums[columns : 2 * columns] += jnp.dot(part_t, part, preferred_element_type=F32)

    moment_phases = reduction(1)
    work[:, 0:columns] = total[0:columns] / total_rows
    ids = lax.broadcasted_iota(jnp.int32, (columns, columns), 0)
    lanes = lax.broadcasted_iota(jnp.int32, (columns, columns), 1)
    work[:, columns : 2 * columns] = (ids == lanes).astype(F32)
    panels = columns // PANEL
    done = 0
    for index, (start, finish) in enumerate(moment_phases):
        start()
        until = (index + 1) * panels // len(moment_phases)
        for p in range(done, until):
            eliminate(work, p)
        done = until
        if index == len(moment_phases) - 1:
            inverse = work[:, columns : 2 * columns]
            inverse_out[...] = inverse
            flipped = inverse.T
            top = flipped.astype(BF16)
            high_out[...] = top
            low_out[...] = (flipped - top.astype(F32)).astype(BF16)
        finish()
    moment_out[...] = total[columns : 2 * columns] / total_rows


def eliminate(work, p):
    order = work.shape[0]
    half = order // 2
    inside = lax.broadcasted_iota(jnp.int32, (PANEL, 1), 0)
    base, end = p * PANEL, (p + 1) * PANEL
    low = (base // half) * half
    top = low + half
    wide = work[base:end, low : order + top]
    column = [
        jnp.broadcast_to(work[base:end, base + k : base + k + 1], (PANEL, 128)) for k in range(PANEL)
    ]
    width = order + top - low
    inverse = []
    for j in range(PANEL):
        pivot = 1.0 / column[j][j : j + 1, :]
        inverse.append(pivot)
        if j < PANEL - 1:
            factor = jnp.where(inside > j, column[j] * pivot, 0.0)
            for k in range(j + 1, PANEL):
                column[k] = column[k] - factor * column[k][j : j + 1, :]
            wide = wide - jnp.tile(factor, (1, width // 128)) * wide[j : j + 1, :]
    inverse = jnp.concatenate(inverse, axis=0)
    if end < order:
        first = (end // half) * half
        scaled = wide[:, first - low : order - low] * jnp.tile(inverse, (1, (order - first) // 128))
        ids = lax.broadcasted_iota(jnp.int32, scaled.shape, 1) + first
        scaled = jnp.where(ids >= end, scaled, 0.0)
        work[first:order, low : order + top] -= lax.dot_general(
            scaled, wide, (((0,), (0,)), ((), ())), precision=HIGHEST, preferred_element_type=F32
        )
    root = jnp.sqrt(inverse)
    work[base:end, order : order + top] = wide[:, order - low :] * jnp.tile(root, (1, top // 128))


def basis_kernel(slab_ref, moment_ref, inverse_ref, high, low, basis_ref, projected_ref):
    @pl.when(pl.program_id(0) == pl.num_programs(0) - 1)
    def _():
        inverse = inverse_ref[...]
        left = jnp.dot(inverse, moment_ref[...], precision=HIGHEST, preferred_element_type=F32)
        projected_ref[...] = lax.dot_general(
            left, inverse, (((1,), (1,)), ((), ())), precision=HIGHEST, preferred_element_type=F32
        )

    slab = slab_ref[...]
    basis_ref[...] = jnp.dot(slab, high[...], preferred_element_type=F32) + jnp.dot(
        slab, low[...], preferred_element_type=F32
    )


def body(start_slab, blocks, couple, counts, send_blocks, center, halfwidth):
    rows, slots, size, _ = blocks.shape
    columns = start_slab.shape[1]
    local = start_slab.shape[0]
    lists = send_blocks.shape[2]
    devices = lax.axis_size("rows")
    total_rows = local * devices
    levels = devices.bit_length() - 1
    anywhere = pl.BlockSpec(memory_space=pl.ANY)
    vmem = pl.BlockSpec(memory_space=pltpu.VMEM)
    own = pltpu.VMEM((rows, size, columns), BF16)
    ext = pltpu.VMEM((rows + 2 * lists, size, columns), BF16)
    listed = pltpu.VMEM((lists, size, columns), BF16)
    table = jnp.concatenate([couple.reshape(-1), counts, send_blocks.reshape(-1)])
    scale = jnp.concatenate([center, 1.0 / halfwidth])
    square = jax.ShapeDtypeStruct((columns, columns), F32)
    half = jax.ShapeDtypeStruct((columns, columns), BF16)
    slab, moment, inverse, high, low = pl.pallas_call(
        functools.partial(filter_kernel, devices, float(total_rows)),
        out_shape=(
            jax.ShapeDtypeStruct((rows, size, columns), BF16),
            square,
            square,
            half,
            half,
        ),
        in_specs=[anywhere, anywhere, vmem, anywhere],
        out_specs=(vmem,) * 5,
        scratch_shapes=[
            pltpu.VMEM(blocks.shape, BF16),
            pltpu.SMEM(table.shape, jnp.int32),
            pltpu.SMEM(scale.shape, F32),
            pltpu.VMEM((columns, 2 * columns), F32),
            own,
            own,
            ext,
            ext,
            listed,
            listed,
            listed,
            listed,
            pltpu.VMEM((columns, local), BF16),
            pltpu.VMEM((2 * columns, columns), F32),
            pltpu.VMEM((2 * columns, columns), F32),
            pltpu.VMEM((2 * columns, columns), F32),
            pltpu.SemaphoreType.DMA,
            pltpu.SemaphoreType.DMA((2,)),
            pltpu.SemaphoreType.DMA((STEPS + 1, 2)),
            pltpu.SemaphoreType.DMA((STEPS + 1, 2)),
            pltpu.SemaphoreType.DMA((2, 2 * levels)),
            pltpu.SemaphoreType.DMA((2, 2 * levels)),
        ],
        compiler_params=pltpu.CompilerParams(
            collective_id=0, has_side_effects=True, vmem_limit_bytes=48 * 1024 * 1024
        ),
    )(
        table,
        scale,
        start_slab.reshape(rows, size, columns),
        blocks,
    )
    tile = 512
    return pl.pallas_call(
        basis_kernel,
        grid=(local // tile,),
        out_shape=(
            jax.ShapeDtypeStruct((local, columns), F32),
            jax.ShapeDtypeStruct((columns, columns), F32),
        ),
        in_specs=[
            pl.BlockSpec((tile, columns), lambda i: (i, 0)),
            *[pl.BlockSpec((columns, columns), lambda i: (0, 0))] * 4,
        ],
        out_specs=(
            pl.BlockSpec((tile, columns), lambda i: (i, 0)),
            pl.BlockSpec((columns, columns), lambda i: (0, 0)),
        ),
        compiler_params=pltpu.CompilerParams(vmem_limit_bytes=32 * 1024 * 1024),
    )(slab.reshape(local, columns), moment, inverse, high, low)


def solution(mesh):
    return jax.shard_map(
        body,
        mesh=mesh,
        in_specs=(
            P(("packs", "rows"), None),
            P(("packs", "rows"), None, None, None),
            P(("packs", "rows"), None),
            P(("packs", "rows")),
            P(("packs", "rows"), None, None),
            P(),
            P(),
        ),
        out_specs=(P(("packs", "rows"), None), P("packs", None)),
        check_vma=False,
    )
```

```python
import functools

import jax
import jax.numpy as jnp
from jax import lax
from jax.experimental import pallas as pl
from jax.experimental.pallas import tpu as pltpu
from jax.sharding import PartitionSpec as P

STEPS = 3
PANEL = 16
PARTS = 2
CHUNK = 512
F32 = jnp.float32
BF16 = jnp.bfloat16
HIGHEST = lax.Precision.HIGHEST


def radices(devices):
    groups = []
    stride = 1
    while stride < devices:
        left = devices // stride
        radix = 4 if (left.bit_length() - 1) % 2 == 0 else 2
        groups.append((stride, radix))
        stride *= radix
    return groups


def filter_kernel(
    devices,
    total_rows,
    couple_hbm,
    counts_hbm,
    send_hbm,
    center_hbm,
    halfwidth_hbm,
    start_hbm,
    blocks_hbm,
    slab_out,
    moment_out,
    inverse_out,
    high_out,
    low_out,
    blocks_ref,
    couple_ref,
    counts_ref,
    send_ref,
    center_ref,
    halfwidth_ref,
    work,
    own_a,
    own_b,
    ext_0,
    ext_1,
    ext_2,
    ext_3,
    up_a,
    up_b,
    down_a,
    down_b,
    slab_t,
    sums,
    arrived,
    total,
    load_sem,
    table_sem,
    send_sem,
    recv_sem,
    sum_send_sem,
    sum_recv_sem,
):
    rows = blocks_ref.shape[0]
    slots = blocks_ref.shape[1]
    size = blocks_ref.shape[2]
    columns = slab_t.shape[0]
    exts = (ext_0, ext_1, ext_2, ext_3)
    lists = (ext_0.shape[0] - rows) // 2
    part = lists // PARTS
    me = lax.axis_index("rows")
    groups_of = radices(devices)

    def peer(stride, radix, turn):
        digit = (me // stride) % radix
        other = (digit + turn) % radix
        return me + stride * (other - digit), other

    load = pltpu.make_async_copy(blocks_hbm, blocks_ref, load_sem)
    tables = (
        pltpu.make_async_copy(start_hbm, own_a, table_sem.at[0]),
        pltpu.make_async_copy(start_hbm, ext_0.at[pl.ds(0, rows)], table_sem.at[1]),
        pltpu.make_async_copy(send_hbm, send_ref, table_sem.at[2]),
        pltpu.make_async_copy(couple_hbm, couple_ref, table_sem.at[3]),
        pltpu.make_async_copy(counts_hbm, counts_ref, table_sem.at[4]),
        pltpu.make_async_copy(center_hbm, center_ref, table_sem.at[5]),
        pltpu.make_async_copy(halfwidth_hbm, halfwidth_ref, table_sem.at[6]),
    )
    for copy in tables:
        copy.start()
    load.start()

    barrier = pltpu.get_barrier_semaphore()

    @pl.when(me > 0)
    def _():
        pl.semaphore_signal(barrier, inc=1, device_id={"rows": me - 1}, device_id_type=pl.DeviceIdType.MESH)

    @pl.when(me < devices - 1)
    def _():
        pl.semaphore_signal(barrier, inc=1, device_id={"rows": me + 1}, device_id_type=pl.DeviceIdType.MESH)

    for stride, radix in groups_of:
        for turn in range(1, radix):
            pl.semaphore_signal(
                barrier,
                inc=1,
                device_id={"rows": peer(stride, radix, turn)[0]},
                device_id_type=pl.DeviceIdType.MESH,
            )

    for ext in exts:
        @pl.when(me == 0)
        def _():
            ext[rows : rows + lists] = jnp.zeros((lists, size, columns), BF16)

        @pl.when(me == devices - 1)
        def _():
            ext[rows + lists : rows + 2 * lists] = jnp.zeros((lists, size, columns), BF16)

    for copy in tables:
        copy.wait()
    ends = (me == 0).astype(jnp.int32) + (me == devices - 1).astype(jnp.int32)
    pl.semaphore_wait(barrier, sum(radix - 1 for _, radix in groups_of) + 2 - ends)

    def exchange(step):
        ext = exts[step]
        sides = (
            ((down_a, down_b)[step % 2], rows + lists, me - 1),
            ((up_a, up_b)[step % 2], rows, me + 1),
        )
        copies = [
            [
                pltpu.make_async_remote_copy(
                    src_ref=listed.at[pl.ds(c * part, part)],
                    dst_ref=ext.at[pl.ds(first + c * part, part)],
                    send_sem=send_sem.at[step, side, c],
                    recv_sem=recv_sem.at[step, side, c],
                    device_id={"rows": target},
                    device_id_type=pl.DeviceIdType.MESH,
                )
                for c in range(PARTS)
            ]
            for side, (listed, first, target) in enumerate(sides)
        ]
        open_sides = (me > 0, me < devices - 1)

        def start(make):
            for c in range(PARTS):
                for side in (1, 0):
                    @pl.when(open_sides[side])
                    def _():
                        @pl.loop(c * part, (c + 1) * part)
                        def _(j):
                            sides[side][0][j] = make(send_ref[side, j])

                        copies[side][c].start()

        def finish():
            for side in range(2):
                @pl.when(open_sides[side])
                def _():
                    for c in range(PARTS):
                        copies[side][c].wait_send()
                        copies[1 - side][c].wait_recv()

        return start, finish

    def conduct(ext, r):
        live = counts_ref[r]
        left, right = [], []
        for k in range(slots):
            block = blocks_ref[r, k]
            left.append(jnp.where(k < live, block, jnp.zeros_like(block)))
            right.append(ext[couple_ref[k, r]])
        return jnp.dot(
            jnp.concatenate(left, axis=1), jnp.concatenate(right, axis=0), preferred_element_type=F32
        )

    def reduction(which):
        phases = []
        spans = []
        offset = which * columns
        length = columns
        at = which * columns
        flag = 0
        for index, (stride, radix) in enumerate(groups_of):
            length //= radix
            copies = []
            for turn in range(1, radix):
                other, digit = peer(stride, radix, turn)
                give = pl.multiple_of(offset + digit * length, length)
                copies.append(
                    pltpu.make_async_remote_copy(
                        src_ref=sums.at[pl.ds(give, length)],
                        dst_ref=arrived.at[pl.ds(at + (turn - 1) * length, length)],
                        send_sem=sum_send_sem.at[which, flag],
                        recv_sem=sum_recv_sem.at[which, flag],
                        device_id={"rows": other},
                        device_id_type=pl.DeviceIdType.MESH,
                    )
                )
                flag += 1
            keep = pl.multiple_of(offset + (me // stride) % radix * length, length)

            def start(copies=copies):
                for copy in copies:
                    copy.start()

            def finish(copies=copies, keep=keep, at=at, length=length, last=index == len(groups_of) - 1):
                here = sums[pl.ds(keep, length)]
                for turn, copy in enumerate(copies):
                    copy.wait()
                    here += arrived[pl.ds(at + turn * length, length)]
                (total if last else sums)[pl.ds(keep, length)] = here

            phases.append((start, finish))
            spans.append((keep, length))
            offset = keep
            at += (radix - 1) * length
        for (stride, radix), (keep, length) in zip(reversed(groups_of), reversed(spans)):
            copies = []
            for turn in range(1, radix):
                copies.append(
                    pltpu.make_async_remote_copy(
                        src_ref=total.at[pl.ds(keep, length)],
                        dst_ref=total.at[pl.ds(keep, length)],
                        send_sem=sum_send_sem.at[which, flag],
                        recv_sem=sum_recv_sem.at[which, flag],
                        device_id={"rows": peer(stride, radix, turn)[0]},
                        device_id_type=pl.DeviceIdType.MESH,
                    )
                )
                flag += 1

            def start(copies=copies):
                for copy in copies:
                    copy.start()

            def finish(copies=copies):
                for copy in copies:
                    copy.wait()

            phases.append((start, finish))
        return phases

    start, finish = exchange(0)
    start(lambda r: own_a[r])
    load.wait()
    for step in range(STEPS):
        ext, ext_next = exts[step], exts[step + 1]
        own, own_next = ((own_a, own_b), (own_b, own_a))[step % 2]
        inverse = 1.0 / jnp.full((1, columns), halfwidth_ref[step], F32)

        def apply(r):
            product = conduct(ext, r)
            return ((product - center_ref[step] * own[r].astype(F32)) * inverse).astype(BF16)

        finish()
        start, finish = exchange(step + 1)
        start(apply)

        @pl.loop(0, rows)
        def _(r):
            new = apply(r)
            own_next[r] = new
            ext_next[r] = new

    own, image = ((own_a, own_b), (own_b, own_a))[STEPS % 2]
    ext = exts[STEPS]
    sums[...] = jnp.zeros_like(sums)
    per = CHUNK // size

    @pl.loop(0, rows // per)
    def _(c):
        part = own[pl.ds(c * per, per)].reshape(CHUNK, columns)
        part_t = part.T
        slab_t[:, pl.ds(pl.multiple_of(c * CHUNK, CHUNK), CHUNK)] = part_t
        sums[0:columns] += jnp.dot(part_t, part, preferred_element_type=F32)
        slab_out[pl.ds(c * per, per)] = own[pl.ds(c * per, per)]

    gram_phases = reduction(0)
    gram_phases[0][0]()
    gram_phases[0][1]()
    gram_phases[1][0]()
    finish()
    groups = len(gram_phases) - 1
    for group in range(groups):
        @pl.loop(group * rows // groups, (group + 1) * rows // groups)
        def _(r):
            image[r] = conduct(ext, r).astype(BF16)

        gram_phases[group + 1][1]()
        if group < groups - 1:
            gram_phases[group + 2][0]()

    @pl.loop(0, rows // per)
    def _(c):
        part = image[pl.ds(c * per, per)].reshape(CHUNK, columns)
        part_t = slab_t[:, pl.ds(pl.multiple_of(c * CHUNK, CHUNK), CHUNK)]
        sums[columns : 2 * columns] += jnp.dot(part_t, part, preferred_element_type=F32)

    moment_phases = reduction(1)
    work[:, 0:columns] = total[0:columns] / total_rows
    ids = lax.broadcasted_iota(jnp.int32, (columns, columns), 0)
    lanes = lax.broadcasted_iota(jnp.int32, (columns, columns), 1)
    work[:, columns : 2 * columns] = (ids == lanes).astype(F32)
    panels = columns // PANEL
    done = 0
    for index, (start, finish) in enumerate(moment_phases):
        start()
        until = (index + 1) * panels // len(moment_phases)
        for p in range(done, until):
            pl.when(me >= 0)(functools.partial(eliminate, work, p))
        done = until
        if index == len(moment_phases) - 1:
            inverse = work[:, columns : 2 * columns]
            inverse_out[...] = inverse
            flipped = inverse.T
            top = flipped.astype(BF16)
            high_out[...] = top
            low_out[...] = (flipped - top.astype(F32)).astype(BF16)
        finish()
    moment_out[...] = total[columns : 2 * columns] / total_rows


def eliminate(work, p):
    order = work.shape[0]
    half = order // 2
    inside = lax.broadcasted_iota(jnp.int32, (PANEL, 1), 0)
    base, end = p * PANEL, (p + 1) * PANEL
    low = (base // half) * half
    top = low + half
    wide = work[base:end, low : order + top]
    column = [
        jnp.broadcast_to(work[base:end, base + k : base + k + 1], (PANEL, 128)) for k in range(PANEL)
    ]
    width = order + top - low
    inverse = []
    for j in range(PANEL):
        pivot = 1.0 / column[j][j : j + 1, :]
        inverse.append(pivot)
        if j < PANEL - 1:
            factor = jnp.where(inside > j, column[j] * pivot, 0.0)
            for k in range(j + 1, PANEL):
                column[k] = column[k] - factor * column[k][j : j + 1, :]
            wide = wide - jnp.tile(factor, (1, width // 128)) * wide[j : j + 1, :]
    inverse = jnp.concatenate(inverse, axis=0)
    if end < order:
        first = (end // half) * half
        scaled = wide[:, first - low : order - low] * jnp.tile(inverse, (1, (order - first) // 128))
        ids = lax.broadcasted_iota(jnp.int32, scaled.shape, 1) + first
        scaled = jnp.where(ids >= end, scaled, 0.0)
        work[first:order, low : order + top] -= lax.dot_general(
            scaled, wide, (((0,), (0,)), ((), ())), precision=HIGHEST, preferred_element_type=F32
        )
    root = jnp.sqrt(inverse)
    work[base:end, order : order + top] = wide[:, order - low :] * jnp.tile(root, (1, top // 128))


def basis_kernel(slab_ref, moment_ref, inverse_ref, high, low, basis_ref, projected_ref):
    @pl.when(pl.program_id(0) == pl.num_programs(0) - 1)
    def _():
        inverse = inverse_ref[...]
        left = jnp.dot(inverse, moment_ref[...], precision=HIGHEST, preferred_element_type=F32)
        projected_ref[...] = lax.dot_general(
            left, inverse, (((1,), (1,)), ((), ())), precision=HIGHEST, preferred_element_type=F32
        )

    slab = slab_ref[...]
    basis_ref[...] = jnp.dot(slab, high[...], preferred_element_type=F32) + jnp.dot(
        slab, low[...], preferred_element_type=F32
    )


def body(start_slab, blocks, couple, counts, send_blocks, center, halfwidth):
    rows, slots, size, _ = blocks.shape
    columns = start_slab.shape[1]
    local = start_slab.shape[0]
    lists = send_blocks.shape[2]
    devices = lax.axis_size("rows")
    total_rows = local * devices
    flags = 2 * sum(radix - 1 for _, radix in radices(devices))
    anywhere = pl.BlockSpec(memory_space=pltpu.HBM)
    vmem = pl.BlockSpec(memory_space=pltpu.VMEM)
    own = pltpu.VMEM((rows, size, columns), BF16)
    ext = pltpu.VMEM((rows + 2 * lists, size, columns), BF16)
    listed = pltpu.VMEM((lists, size, columns), BF16)
    square = jax.ShapeDtypeStruct((columns, columns), F32)
    half = jax.ShapeDtypeStruct((columns, columns), BF16)
    slab, moment, inverse, high, low = pl.pallas_call(
        functools.partial(filter_kernel, devices, float(total_rows)),
        out_shape=(
            jax.ShapeDtypeStruct((rows, size, columns), BF16),
            square,
            square,
            half,
            half,
        ),
        in_specs=[anywhere] * 7,
        out_specs=(vmem,) * 5,
        scratch_shapes=[
            pltpu.VMEM(blocks.shape, BF16),
            pltpu.SMEM((slots, rows), jnp.int32),
            pltpu.SMEM((rows,), jnp.int32),
            pltpu.SMEM((2, lists), jnp.int32),
            pltpu.SMEM((STEPS,), F32),
            pltpu.SMEM((STEPS,), F32),
            pltpu.VMEM((columns, 2 * columns), F32),
            own,
            own,
            *[ext] * (STEPS + 1),
            listed,
            listed,
            listed,
            listed,
            pltpu.VMEM((columns, local), BF16),
            pltpu.VMEM((2 * columns, columns), F32),
            pltpu.VMEM((2 * columns, columns), F32),
            pltpu.VMEM((2 * columns, columns), F32),
            pltpu.SemaphoreType.DMA,
            pltpu.SemaphoreType.DMA((7,)),
            pltpu.SemaphoreType.DMA((STEPS + 1, 2, PARTS)),
            pltpu.SemaphoreType.DMA((STEPS + 1, 2, PARTS)),
            pltpu.SemaphoreType.DMA((2, flags)),
            pltpu.SemaphoreType.DMA((2, flags)),
        ],
        compiler_params=pltpu.CompilerParams(
            collective_id=0, has_side_effects=True, vmem_limit_bytes=48 * 1024 * 1024
        ),
    )(
        couple.T,
        counts,
        send_blocks[0],
        center,
        halfwidth,
        start_slab.reshape(rows, size, columns),
        blocks,
    )
    tile = 512
    return pl.pallas_call(
        basis_kernel,
        grid=(local // tile,),
        out_shape=(
            jax.ShapeDtypeStruct((local, columns), F32),
            jax.ShapeDtypeStruct((columns, columns), F32),
        ),
        in_specs=[
            pl.BlockSpec((tile, columns), lambda i: (i, 0)),
            *[pl.BlockSpec((columns, columns), lambda i: (0, 0))] * 4,
        ],
        out_specs=(
            pl.BlockSpec((tile, columns), lambda i: (i, 0)),
            pl.BlockSpec((columns, columns), lambda i: (0, 0)),
        ),
        compiler_params=pltpu.CompilerParams(vmem_limit_bytes=32 * 1024 * 1024),
    )(slab.reshape(local, columns), moment, inverse, high, low)


def solution(mesh):
    return jax.shard_map(
        body,
        mesh=mesh,
        in_specs=(
            P(("packs", "rows"), None),
            P(("packs", "rows"), None, None, None),
            P(("packs", "rows"), None),
            P(("packs", "rows")),
            P(("packs", "rows"), None, None),
            P(),
            P(),
        ),
        out_specs=(P(("packs", "rows"), None), P("packs", None)),
        check_vma=False,
    )
```
